768 devices in a mesh: row: 4 (over z_hi, core), col: 24 (over x, z_lo), ri: 8 (over y).
Axes of the slice: x: 4, y: 8, z: 12 (z_hi: 2, z_lo: 6; z = z_hi * 6 + z_lo), core: 2. Of those that a mesh axis runs over, the one named last changes fastest.
Arguments:
- coulomb3: bfloat16 [768, 768, 768], P(('row', 'ri'), 'col'), may hold values from -6 to 6
- tile_mask: int32 [24, 24], replicated, may hold values from 0 to 1, as said below
- tile_fill: int32 [24], replicated, may hold values from 16 to 32, as said below
- occ_density: bfloat16 [768, 768], P('col'), may hold values from -0.21875 to 0.21875
- virt_density: bfloat16 [768, 768], P('col'), may hold values from -0.21875 to 0.21875
Outputs:
- transformed: bfloat16 [32, 24, 768, 768], P(('row', 'ri'), 'col')
The draws below stay inside these ranges and needn't reach their ends.
Inputs may be any that keep to these rules, and one draw needn't show every extreme that they name: tile_mask[a, b] is 1 where atom blocks a and b pass screening; it is symmetric and 1 on the diagonal. tile_fill[t] counts the basis functions of tile t, which occupy its first positions; the rest is padding. Some tile is full and some tile holds exactly 16.
All inputs are finite; a program needn't handle non-finite values.
Results may differ from the reference program's by a relative error of at most 0.0049.
Values may be sent and summed in bfloat16 or wider, within the bound.
A program may use at most 32 MiB of HBM per device.

```python
import jax
import jax.numpy as jnp
from jax import lax

BS = 32
P_DEV = 24
NTILE = 24
NORB = 768
PGROUPS = 32
NRI = 768


def draw_tile_mask(key, part):
    key = jax.random.fold_in(key, 11)
    key_score, key_level, key_pick, key_other = jax.random.split(key, 4)
    scores = jax.random.randint(key_score, (NTILE, NTILE), 0, 100)
    levels = jax.random.randint(key_level, (NTILE, 1), 10, 70)
    passed = (scores < levels).astype(jnp.int32)
    passed = jnp.maximum(passed, passed.T)
    pick_one = jax.random.randint(key_pick, (), 0, NTILE)
    pick_two = (pick_one + 1 + jax.random.randint(key_other, (), 0, NTILE - 1)) % NTILE
    row_ids = jnp.arange(NTILE)[:, None]
    col_ids = jnp.arange(NTILE)[None, :]
    broken = (row_ids == pick_one) & (col_ids == pick_two) | (row_ids == pick_two) & (col_ids == pick_one)
    passed = jnp.where(broken, 0, passed)
    diagonal = (row_ids == col_ids).astype(jnp.int32)
    return jnp.maximum(passed, diagonal).astype(jnp.int32)


def draw_tile_fill(key, part):
    key = jax.random.fold_in(key, 23)
    key_fill, key_full = jax.random.split(key)
    counts = jax.random.randint(key_fill, (NTILE,), BS // 2, BS + 1)
    full_at = jax.random.randint(key_full, (), 0, NTILE)
    half_at = (full_at + 1) % NTILE
    tile_ids = jnp.arange(NTILE)
    counts = jnp.where(tile_ids == half_at, BS // 2, counts)
    return jnp.where(tile_ids == full_at, BS, counts).astype(jnp.int32)


def steps_of(key, dims, cuts, low, largest):
    def one(dim, parts):
        heights = jax.random.uniform(jax.random.fold_in(jax.random.fold_in(key, 6), dim), (parts,), jnp.float32, low / len(cuts), largest / len(cuts))
        return jnp.repeat(jnp.exp(heights), dims[dim] // parts).reshape((-1,) + (1,) * (len(dims) - dim - 1))

    gain = one(*cuts[0])
    for cut in cuts[1:]:
        gain = gain * one(*cut)
    return gain


def normal_values(stream_key, shape, spread, most, cuts=(), kind=jnp.bfloat16):
    values = jax.random.normal(stream_key, shape, jnp.float32) * spread
    if len(cuts) > 0:
        values = steps_of(stream_key, shape, cuts, -0.22, 0.18) * values
    return jnp.clip(values, min=-most, max=most).astype(kind)


def setup_inputs(seed: int = 0) -> dict:
    arg_keys = jax.random.split(jax.random.key(seed), 6)
    return {
        "coulomb3": normal_values(arg_keys[0], (NRI, NORB, NORB), 1.0, 6.0, ((0, 32), (1, 24))),
        "tile_mask": draw_tile_mask(jax.random.fold_in(arg_keys[5], 71), 0),
        "tile_fill": draw_tile_fill(jax.random.fold_in(arg_keys[5], 71), 0),
        "occ_density": normal_values(arg_keys[3], (NORB, NORB), NORB ** -0.5, 0.21875, ((0, 24),)),
        "virt_density": normal_values(arg_keys[4], (NORB, NORB), NORB ** -0.5, 0.21875, ((0, 24),)),
    }


def reference(coulomb3, tile_mask, tile_fill, occ_density, virt_density):
    positions = jnp.arange(NORB, dtype=jnp.int32)
    tile_of = positions // BS
    live = (positions % BS < tile_fill[tile_of]).astype(jnp.int32)
    pair = tile_mask[tile_of][:, tile_of] * live[:, None] * live[None, :]
    weight = pair.astype(jnp.bfloat16)
    live_float = live.astype(jnp.float32)
    occ_wide = occ_density.astype(jnp.float32)
    virt_wide = virt_density.astype(jnp.float32)

    def one_group(slab):
        screened = slab * weight[None]
        half_trans = jnp.einsum("pmn,ns->pms", screened.astype(jnp.float32), occ_wide).astype(jnp.bfloat16)
        product = jnp.einsum("lm,pms->pls", virt_wide, half_trans.astype(jnp.float32))
        return (product * live_float[None, :, None] * live_float[None, None, :]).astype(jnp.bfloat16)

    groups = coulomb3.reshape(PGROUPS, P_DEV, NORB, NORB)
    return lax.map(one_group, groups)
```

```python
import functools

import jax
import jax.numpy as jnp
from jax import lax
from jax.experimental import pallas as pl
from jax.experimental.pallas import tpu as pltpu
from jax.sharding import PartitionSpec as P

MESH = pl.DeviceIdType.MESH
NX, NZ, NY = 4, 6, 8
BS, NTILE, NORB = 32, 24, 768
SLABS = NORB // 128
GROUP = NZ * BS


def gather_kernel(
    width, fill_ref, mask_ref, c_hbm, o_hbm, v_hbm, h_ref, vm_ref,
    c_in, c_out, c_got, own, full, pick, occ,
    load_sem, send_sem, recv_sem, z_send, z_recv, y_send, y_recv, x_send, x_recv, k_send, k_recv,
):
    row, col, y = lax.axis_index("row"), lax.axis_index("col"), lax.axis_index("ri")
    x, z = col // NZ, col % NZ
    core = row % 2
    other = row + 1 - 2 * core

    loads = [
        pltpu.make_async_copy(o_hbm, own.at[0], load_sem.at[0]),
        pltpu.make_async_copy(v_hbm, own.at[1], load_sem.at[1]),
        pltpu.make_async_copy(c_hbm, c_in, load_sem.at[2]),
    ]
    for load in loads:
        load.start()

    barrier = pltpu.get_barrier_semaphore()

    def greet_col(d, _):
        pl.semaphore_signal(barrier, inc=1, device_id={"col": (col + d) % NTILE}, device_id_type=MESH)
        return 0

    def greet_y(d, _):
        pl.semaphore_signal(barrier, inc=1, device_id={"ri": (y + d) % NY}, device_id_type=MESH)
        return 0

    lax.fori_loop(1, NTILE, greet_col, 0)
    lax.fori_loop(1, NY, greet_y, 0)
    pl.semaphore_signal(barrier, inc=1, device_id={"row": other}, device_id_type=MESH)

    place = lax.broadcasted_iota(jnp.int32, (8, NORB), 1)
    tile, pos = place // BS, place % BS
    rank = jnp.full((8, NORB), -1, jnp.int32)
    weight = jnp.zeros((8, NORB), jnp.int32)
    offset = jnp.int32(0)
    for t in range(NTILE):
        here = (tile == t) & (pos < fill_ref[t])
        rank = jnp.where(here, pos + offset, rank)
        weight = jnp.where(here, mask_ref[col, t], weight)
        offset = offset + fill_ref[t]
    live = (rank >= 0).astype(jnp.float32)[:1]
    weight = weight.astype(jnp.float32)[:1]

    def build(i, _):
        rows = pl.ds(i * 128, 128)
        want = lax.broadcasted_iota(jnp.int32, (128, NORB), 0) + i * 128
        pick[rows, :] = (rank[:1] == want).astype(jnp.float32).astype(jnp.bfloat16)
        return 0

    lax.fori_loop(0, width // 128, build, 0)

    live_rows = lax.broadcasted_iota(jnp.int32, (BS, 1), 0) < fill_ref[col]
    screen = (weight * live_rows.astype(jnp.float32)).astype(jnp.bfloat16)
    loads[2].wait()

    def pack(i, _):
        block = (c_in[:, i] * screen[None]).reshape(NX * BS, NORB)
        packed = lax.dot_general(block, pick[...], (((1,), (1,)), ((), ())), preferred_element_type=jnp.float32)
        c_out[i] = packed.astype(jnp.bfloat16).reshape(NX, BS, width)
        return 0

    lax.fori_loop(0, NZ, pack, 0)
    loads[0].wait()
    loads[1].wait()
    pl.semaphore_wait(barrier, NTILE + NY - 1)

    def z_copy(to, at):
        rows = pl.ds(x * GROUP + at * BS, BS)
        cols = pl.ds(pl.multiple_of(y * 128, 128), 128)
        return pltpu.make_async_remote_copy(
            src_ref=own.at[core, :, cols], dst_ref=full.at[core, rows, cols],
            send_sem=z_send.at[to], recv_sem=z_recv.at[at],
            device_id={"col": x * NZ + to}, device_id_type=MESH,
        )

    def own_z():
        cols = pl.ds(pl.multiple_of(y * 128, 128), 128)
        return pltpu.make_async_copy(own.at[core, :, cols], full.at[core, pl.ds(col * BS, BS), cols], load_sem.at[0])

    def y_copy(to, at):
        rows = pl.ds(x * GROUP, GROUP)
        cols = pl.ds(pl.multiple_of(at * 128, 128), 128)
        return pltpu.make_async_remote_copy(
            src_ref=full.at[core, rows, cols], dst_ref=full.at[core, rows, cols],
            send_sem=y_send.at[to], recv_sem=y_recv.at[at],
            device_id={"ri": to}, device_id_type=MESH,
        )

    def x_copy(to, at):
        rows = pl.ds(at * GROUP, GROUP)
        return pltpu.make_async_remote_copy(
            src_ref=full.at[core, rows], dst_ref=full.at[core, rows],
            send_sem=x_send.at[to], recv_sem=x_recv.at[at],
            device_id={"col": to * NZ + z}, device_id_type=MESH,
        )

    def k_copy(part, at):
        rows = pl.ds(part * GROUP, GROUP)
        return pltpu.make_async_remote_copy(
            src_ref=full.at[at, rows], dst_ref=full.at[at, rows],
            send_sem=k_send.at[part], recv_sem=k_recv.at[part],
            device_id={"row": other}, device_id_type=MESH,
        )

    def c_copy(to_x, to_z, at_x, at_z):
        return pltpu.make_async_remote_copy(
            src_ref=c_out.at[to_z, to_x], dst_ref=c_got.at[at_z, at_x],
            send_sem=send_sem.at[to_z, to_x], recv_sem=recv_sem.at[at_z, at_x],
            device_id={"col": to_x * NZ + to_z}, device_id_type=MESH,
        )

    @pl.when(y < SLABS)
    def _():
        def send(d, _):
            z_copy((z + d) % NZ, z).start()
            return 0

        own_z().start()
        lax.fori_loop(1, NZ, send, 0)

    half = z // 3
    keep = pltpu.make_async_copy(c_out.at[z, x], c_got.at[z, x], load_sem.at[2])
    keep.start()

    def send_tile(i, _):
        to_z = (i + 3 * (1 - half)) % NZ

        def send(d, _):
            to_x = (x + d) % NX

            @pl.when((d > 0) | (to_z != z))
            def _():
                c_copy(to_x, to_z, x, z).start()

            return 0

        return lax.fori_loop(0, NX, send, 0)

    lax.fori_loop(0, NZ, send_tile, 0)

    @pl.when(y < SLABS)
    def _():
        def take(d, _):
            z_copy(z, (z + d) % NZ).wait_recv()
            return 0

        def send(d, _):
            y_copy((y + d) % NY, y).start()
            return 0

        own_z().wait()
        lax.fori_loop(1, NZ, take, 0)
        lax.fori_loop(1, NY, send, 0)

    def take_y(s, _):
        @pl.when(y != s)
        def _():
            y_copy(y, s).wait_recv()

        return 0

    lax.fori_loop(0, SLABS, take_y, 0)

    def send_x(d, _):
        x_copy((x + d) % NX, x).start()
        return 0

    lax.fori_loop(1, NX, send_x, 0)
    k_copy(x, core).start()

    def take_x(d, _):
        part = (x + d) % NX
        x_copy(x, part).wait_recv()
        k_copy(part, core).start()
        return 0

    lax.fori_loop(1, NX, take_x, 0)

    def take_k(part, _):
        k_copy(part, 1 - core).wait_recv()
        return 0

    lax.fori_loop(0, NX, take_k, 0)

    def pack_occ(i, _):
        rows = pl.ds(i * 128, 128)
        packed = jnp.dot(pick[rows, :], full[0], preferred_element_type=jnp.float32)
        occ[rows, :] = (packed * live).astype(jnp.bfloat16)
        return 0

    lax.fori_loop(0, width // 128, pack_occ, 0)

    for t in range(NTILE):
        rows = pl.ds(t * BS, BS)
        alive = lax.broadcasted_iota(jnp.int32, (BS, NORB), 0) < fill_ref[t]
        vm_ref[rows, :] = jnp.where(alive, full[1, rows, :].astype(jnp.float32), 0.0).astype(jnp.bfloat16)

    keep.wait()

    def transform(i, _):
        at_z = (i + 3 * half) % NZ

        def take(d, _):
            at_x = (x + d) % NX

            @pl.when((d > 0) | (at_z != z))
            def _():
                c_copy(x, z, at_x, at_z).wait_recv()

            return 0

        lax.fori_loop(0, NX, take, 0)
        got = c_got[at_z].reshape(NX * BS, width)
        done = jnp.dot(got, occ[...], preferred_element_type=jnp.float32).astype(jnp.bfloat16)
        for k in range(NX):
            h_ref[pl.ds(k * GROUP + at_z * BS, BS), :] = done[k * BS:(k + 1) * BS]
        return 0

    lax.fori_loop(0, NZ, transform, 0)

    @pl.when(y < SLABS)
    def _():
        def left_z(d, _):
            z_copy((z + d) % NZ, z).wait_send()
            return 0

        def left_y(d, _):
            y_copy((y + d) % NY, y).wait_send()
            return 0

        lax.fori_loop(1, NZ, left_z, 0)
        lax.fori_loop(1, NY, left_y, 0)

    def left_x(d, _):
        x_copy((x + d) % NX, x).wait_send()
        return 0

    def left_k(part, _):
        k_copy(part, core).wait_send()
        return 0

    def left_c(i, _):
        to_z, to_x = i // NX, i % NX

        @pl.when((to_z != z) | (to_x != x))
        def _():
            c_copy(to_x, to_z, x, z).wait_send()

        return 0

    lax.fori_loop(1, NX, left_x, 0)
    lax.fori_loop(0, NX, left_k, 0)
    lax.fori_loop(0, NTILE, left_c, 0)


def gather(width, coulomb3, tile_mask, tile_fill, occ_density, virt_density):
    dma = pltpu.SemaphoreType.DMA
    bf16 = jnp.bfloat16
    return pl.pallas_call(
        functools.partial(gather_kernel, width),
        out_shape=[jax.ShapeDtypeStruct((NORB, NORB), bf16)] * 2,
        in_specs=[pl.BlockSpec(memory_space=pltpu.SMEM)] * 2 + [pl.BlockSpec(memory_space=pl.ANY)] * 3,
        out_specs=[pl.BlockSpec(memory_space=pltpu.VMEM)] * 2,
        scratch_shapes=[
            pltpu.VMEM((NX, NZ, BS, NORB), bf16),
            pltpu.VMEM((NZ, NX, BS, width), bf16),
            pltpu.VMEM((NZ, NX, BS, width), bf16),
            pltpu.VMEM((2, BS, NORB), bf16),
            pltpu.VMEM((2, NORB, NORB), bf16),
            pltpu.VMEM((width, NORB), bf16),
            pltpu.VMEM((width, NORB), bf16),
            dma((3,)), dma((NZ, NX)), dma((NZ, NX)), dma((NZ,)), dma((NZ,)),
            dma((NY,)), dma((NY,)), dma((NX,)), dma((NX,)), dma((NX,)), dma((NX,)),
        ],
        compiler_params=pltpu.CompilerParams(
            collective_id=width // 64, has_side_effects=True, vmem_limit_bytes=40 * 1024 * 1024
        ),
        name=f"gather_{width}",
    )(tile_fill, tile_mask, coulomb3.reshape(NX, NZ, BS, NORB), occ_density, virt_density)


def second_kernel(v_ref, h_ref, out_ref):
    out_ref[...] = jnp.dot(v_ref[...], h_ref[...], preferred_element_type=jnp.float32).astype(jnp.bfloat16)


def second(virt, half_trans):
    rows = 256
    return pl.pallas_call(
        second_kernel,
        out_shape=jax.ShapeDtypeStruct((NORB, NORB), jnp.bfloat16),
        grid=(NORB // rows,),
        in_specs=[pl.BlockSpec((rows, NORB), lambda i: (i, 0)), pl.BlockSpec((NORB, NORB), lambda i: (0, 0))],
        out_specs=pl.BlockSpec((rows, NORB), lambda i: (i, 0)),
        name="second",
    )(virt, half_trans)


def on_device(coulomb3, tile_mask, tile_fill, occ_density, virt_density):
    half_trans, virt = gather(NORB, coulomb3, tile_mask, tile_fill, occ_density, virt_density)
    return second(virt, half_trans)[None, None]


def solution(mesh):
    placed = (P(("row", "ri"), "col", None), P(), P(), P("col", None), P("col", None))
    return jax.shard_map(
        on_device,
        mesh=mesh,
        in_specs=placed,
        out_specs=P(("row", "ri"), "col", None, None),
        check_vma=False,
    )
```

```python
import jax
import jax.numpy as jnp
from jax import lax
from jax.experimental import pallas as pl
from jax.experimental.pallas import tpu as pltpu
from jax.sharding import PartitionSpec as P

MESH = pl.DeviceIdType.MESH
NX, NZ, NY = 4, 6, 8
BS, NTILE, NORB = 32, 24, 768
SLABS = NORB // 128
GROUP = NZ * BS
PART = NX * BS


def exchange_kernel(
    fill_hbm, mask_hbm, c_hbm, o_hbm, v_hbm, out_hbm,
    fill_ref, mask_ref, c_in, c_out, c_got, own, full, half_done, done,
    load_sem, send_sem, recv_sem, z_send, z_recv, y_send, y_recv, x_send, x_recv, k_send, k_recv,
):
    row, col, y = lax.axis_index("row"), lax.axis_index("col"), lax.axis_index("ri")
    x, z = col // NZ, col % NZ
    core = row % 2
    other = row + 1 - 2 * core
    half = z // 3

    loads = [
        pltpu.make_async_copy(fill_hbm, fill_ref, load_sem.at[0]),
        pltpu.make_async_copy(mask_hbm, mask_ref, load_sem.at[1]),
        pltpu.make_async_copy(c_hbm, c_in, load_sem.at[2]),
    ]
    for load in loads:
        load.start()

    def load_own(source):
        cols = pl.ds(pl.multiple_of(y * 128, 128), 128)
        return pltpu.make_async_copy(source.at[:, cols], own, load_sem.at[3])

    @pl.when((y < SLABS) & (core == 0))
    def _():
        load_own(o_hbm).start()

    @pl.when((y < SLABS) & (core == 1))
    def _():
        load_own(v_hbm).start()

    barrier = pltpu.get_barrier_semaphore()

    def greet_col(d, _):
        pl.semaphore_signal(barrier, inc=1, device_id={"col": (col + d) % NTILE}, device_id_type=MESH)
        return 0

    def greet_y(d, _):
        pl.semaphore_signal(barrier, inc=1, device_id={"ri": (y + d) % NY}, device_id_type=MESH)
        return 0

    lax.fori_loop(1, NTILE, greet_col, 0)
    lax.fori_loop(1, NY, greet_y, 0)
    pl.semaphore_signal(barrier, inc=1, device_id={"row": other}, device_id_type=MESH)

    loads[0].wait()
    loads[1].wait()
    place = lax.broadcasted_iota(jnp.int32, (8, NORB), 1)
    tile, pos = place // BS, place % BS
    live = jnp.zeros((8, NORB), jnp.int32)
    weight = jnp.zeros((8, NORB), jnp.int32)
    for t in range(NTILE):
        here = (tile == t) & (pos < fill_ref[t])
        live = jnp.where(here, 1, live)
        weight = jnp.where(here, mask_ref[col, t], weight)
    live_cols = live.astype(jnp.float32)[:1]
    live_rows = lax.broadcasted_iota(jnp.int32, (BS, 1), 0) < fill_ref[col]
    screen = (weight.astype(jnp.float32)[:1] * live_rows.astype(jnp.float32)).astype(jnp.bfloat16)

    def out_tile(i):
        turn, odd = i // 2, i % 2
        return (z + turn + odd) % 3 + 3 * ((half + 1 + odd) % 2)

    def in_tile(i):
        turn, odd = i // 2, i % 2
        return (z + 5 - turn + odd) % 3 + 3 * ((half + odd) % 2)

    def pack(i):
        at = out_tile(i)
        c_out[at] = c_in[:, at] * screen[None]

    def z_copy(to, at):
        rows = pl.ds(x * GROUP + at * BS, BS)
        return pltpu.make_async_remote_copy(
            src_ref=own, dst_ref=full.at[core, y, rows],
            send_sem=z_send.at[to], recv_sem=z_recv.at[at],
            device_id={"col": x * NZ + to}, device_id_type=MESH,
        )

    def own_z():
        return pltpu.make_async_copy(own, full.at[core, y, pl.ds(col * BS, BS)], load_sem.at[0])

    def y_copy(to, at):
        rows = pl.ds(x * GROUP, GROUP)
        return pltpu.make_async_remote_copy(
            src_ref=full.at[core, at, rows], dst_ref=full.at[core, at, rows],
            send_sem=y_send.at[to], recv_sem=y_recv.at[at],
            device_id={"ri": to}, device_id_type=MESH,
        )

    def x_copy(to, at, slab):
        rows = pl.ds(at * GROUP, GROUP)
        return pltpu.make_async_remote_copy(
            src_ref=full.at[core, slab, rows], dst_ref=full.at[core, slab, rows],
            send_sem=x_send.at[to, slab], recv_sem=x_recv.at[at, slab],
            device_id={"col": to * NZ + z}, device_id_type=MESH,
        )

    def k_copy(part, at, slab):
        rows = pl.ds(part * GROUP, GROUP)
        return pltpu.make_async_remote_copy(
            src_ref=full.at[at, slab, rows], dst_ref=full.at[at, slab, rows],
            send_sem=k_send.at[part, slab], recv_sem=k_recv.at[part, slab],
            device_id={"row": other}, device_id_type=MESH,
        )

    def slab_at(turn):
        odd = turn % 2
        return (y + odd * (turn + 1) // 2 + (1 - odd) * (NY - turn // 2)) % NY

    def c_copy(to_x, to_z, at_x, at_z):
        return pltpu.make_async_remote_copy(
            src_ref=c_out.at[to_z, to_x], dst_ref=c_got.at[at_z, at_x],
            send_sem=send_sem.at[to_z, to_x], recv_sem=recv_sem.at[at_z, at_x],
            device_id={"col": to_x * NZ + to_z}, device_id_type=MESH,
        )

    def send_tile(i):
        to_z = out_tile(i)

        def send(d, _):
            to_x = (x + d) % NX

            @pl.when((d > 0) | (to_z != z))
            def _():
                c_copy(to_x, to_z, x, z).start()

            return 0

        lax.fori_loop(0, NX, send, 0)

    loads[2].wait()
    lax.fori_loop(0, NZ, lambda i, _: (pack(i), 0)[1], 0)
    pl.semaphore_wait(barrier, NTILE + NY - 1)

    @pl.when(y < SLABS)
    def _():
        def send(d, _):
            z_copy((z + d) % NZ, z).start()
            return 0

        load_own(o_hbm).wait()
        own_z().start()
        lax.fori_loop(1, NZ, send, 0)

    lax.fori_loop(0, NZ, lambda i, _: (send_tile(i), 0)[1], 0)
    keep = pltpu.make_async_copy(c_out.at[z, x], c_got.at[z, x], load_sem.at[1])
    keep.start()

    @pl.when(y < SLABS)
    def _():
        def take(d, _):
            z_copy(z, (z + d) % NZ).wait_recv()
            return 0

        def send(d, _):
            y_copy((y + d) % NY, y).start()
            return 0

        own_z().wait()
        lax.fori_loop(1, NZ, take, 0)
        lax.fori_loop(1, NY, send, 0)

    def spread(turn, _):
        slab = slab_at(turn)

        @pl.when(slab < SLABS)
        def _():
            @pl.when(turn > 0)
            def _():
                y_copy(y, slab).wait_recv()

            def send(d, _):
                x_copy((x + d) % NX, x, slab).start()
                return 0

            lax.fori_loop(1, NX, send, 0)
            k_copy(x, core, slab).start()

        return 0

    lax.fori_loop(0, NY, spread, 0)

    def share(turn, _):
        slab = slab_at(turn)

        @pl.when(slab < SLABS)
        def _():
            def take(d, _):
                part = (x + d) % NX
                x_copy(x, part, slab).wait_recv()
                k_copy(part, core, slab).start()
                return 0

            lax.fori_loop(1, NX, take, 0)

        return 0

    lax.fori_loop(0, NY, share, 0)

    def take_k(which):
        def take(i, _):
            k_copy(i // SLABS, which, i % SLABS).wait_recv()
            return 0

        lax.fori_loop(0, NX * SLABS, take, 0)

    @pl.when(core == 1)
    def _():
        take_k(0)

    occ = jnp.concatenate([full[0, slab] for slab in range(SLABS)], axis=1)
    keep.wait()

    def half_transform(i, _):
        at_z = in_tile(i)

        def take(d, _):
            at_x = (x + d) % NX

            @pl.when((d > 0) | (at_z != z))
            def _():
                c_copy(x, z, at_x, at_z).wait_recv()

            return 0

        lax.fori_loop(0, NX, take, 0)
        got = c_got[at_z].reshape(PART, NORB)
        done = jnp.dot(got, occ, preferred_element_type=jnp.float32).astype(jnp.bfloat16)
        for k in range(NX):
            half_done[pl.ds(k * GROUP + at_z * BS, BS), :] = done[k * BS:(k + 1) * BS]
        return 0

    lax.fori_loop(0, NZ, half_transform, 0)

    @pl.when(core == 0)
    def _():
        take_k(1)

    def store(k):
        rows = pl.ds(k * GROUP, GROUP)
        return pltpu.make_async_copy(done.at[rows], out_hbm.at[rows], load_sem.at[k])

    for k in range(NORB // GROUP):
        rows = pl.ds(k * GROUP, GROUP)
        virt = jnp.concatenate([full[1, slab, rows] for slab in range(SLABS)], axis=1)
        product = jnp.dot(virt, half_done[...], preferred_element_type=jnp.float32) * live_cols
        for t in range(NZ):
            at = lax.broadcasted_iota(jnp.int32, (BS, NORB), 0)
            kept = jnp.where(at < fill_ref[k * NZ + t], product[t * BS:(t + 1) * BS], 0.0)
            done[pl.ds(k * GROUP + t * BS, BS), :] = kept.astype(jnp.bfloat16)
        store(k).start()

    @pl.when(y < SLABS)
    def _():
        def left_z(d, _):
            z_copy((z + d) % NZ, z).wait_send()
            return 0

        def left_y(d, _):
            y_copy((y + d) % NY, y).wait_send()
            return 0

        lax.fori_loop(1, NZ, left_z, 0)
        lax.fori_loop(1, NY, left_y, 0)

    def left_slab(slab, _):
        def left_x(d, _):
            x_copy((x + d) % NX, x, slab).wait_send()
            return 0

        def left_k(part, _):
            k_copy(part, core, slab).wait_send()
            return 0

        lax.fori_loop(1, NX, left_x, 0)
        lax.fori_loop(0, NX, left_k, 0)
        return 0

    def left_c(i, _):
        to_z, to_x = i // NX, i % NX

        @pl.when((to_z != z) | (to_x != x))
        def _():
            c_copy(to_x, to_z, x, z).wait_send()

        return 0

    lax.fori_loop(0, SLABS, left_slab, 0)
    lax.fori_loop(0, NTILE, left_c, 0)
    for k in range(NORB // GROUP):
        store(k).wait()


def exchange(coulomb3, tile_mask, tile_fill, occ_density, virt_density):
    dma = pltpu.SemaphoreType.DMA
    bf16 = jnp.bfloat16
    return pl.pallas_call(
        exchange_kernel,
        out_shape=jax.ShapeDtypeStruct((NORB, NORB), bf16),
        in_specs=[pl.BlockSpec(memory_space=pltpu.HBM)] * 5,
        out_specs=pl.BlockSpec(memory_space=pltpu.HBM),
        scratch_shapes=[
            pltpu.SMEM((NTILE,), jnp.int32),
            pltpu.SMEM((NTILE, NTILE), jnp.int32),
            pltpu.VMEM((NX, NZ, BS, NORB), bf16),
            pltpu.VMEM((NZ, NX, BS, NORB), bf16),
            pltpu.VMEM((NZ, NX, BS, NORB), bf16),
            pltpu.VMEM((BS, 128), bf16),
            pltpu.VMEM((2, SLABS, NORB, 128), bf16),
            pltpu.VMEM((NORB, NORB), bf16),
            pltpu.VMEM((NORB, NORB), bf16),
            dma((5,)), dma((NZ, NX)), dma((NZ, NX)), dma((NZ,)), dma((NZ,)),
            dma((NY,)), dma((NY,)),
            dma((NX, SLABS)), dma((NX, SLABS)), dma((NX, SLABS)), dma((NX, SLABS)),
        ],
        compiler_params=pltpu.CompilerParams(
            collective_id=0, has_side_effects=True, vmem_limit_bytes=60 * 1024 * 1024
        ),
        name="exchange",
    )(tile_fill, tile_mask, coulomb3.reshape(NX, NZ, BS, NORB), occ_density, virt_density)


def on_device(coulomb3, tile_mask, tile_fill, occ_density, virt_density):
    return exchange(coulomb3, tile_mask, tile_fill, occ_density, virt_density)[None, None]


def solution(mesh):
    placed = (P(("row", "ri"), "col", None), P(), P(), P("col", None), P("col", None))
    return jax.shard_map(
        on_device,
        mesh=mesh,
        in_specs=placed,
        out_specs=P(("row", "ri"), "col", None, None),
        check_vma=False,
    )
```

```python
import jax
import jax.numpy as jnp
from jax import lax
from jax.experimental import pallas as pl
from jax.experimental.pallas import tpu as pltpu
from jax.sharding import PartitionSpec as P

MESH = pl.DeviceIdType.MESH
NX, NZ, NY = 4, 6, 8
BS, NTILE, NORB = 32, 24, 768
SLABS = NORB // 128
LATE = 4
GROUP = NZ * BS
PART = NX * BS


def exchange_kernel(
    fill_hbm, mask_hbm, c_hbm, o_hbm, v_hbm, out_hbm,
    fill_ref, mask_ref, c_in, c_out, c_got, own, full, half_done, done,
    load_sem, send_sem, recv_sem, z_send, z_recv, y_send, y_recv, x_send, x_recv, k_send, k_recv,
):
    row, col, y = lax.axis_index("row"), lax.axis_index("col"), lax.axis_index("ri")
    x, z = col // NZ, col % NZ
    core = row % 2
    other = row + 1 - 2 * core
    half = z // 3

    loads = [
        pltpu.make_async_copy(fill_hbm, fill_ref, load_sem.at[0]),
        pltpu.make_async_copy(mask_hbm, mask_ref, load_sem.at[1]),
        pltpu.make_async_copy(c_hbm, c_in, load_sem.at[2]),
    ]
    for load in loads:
        load.start()

    def load_own(source):
        cols = pl.ds(pl.multiple_of(y * 128, 128), 128)
        return pltpu.make_async_copy(source.at[:, cols], own, load_sem.at[3])

    @pl.when((y < SLABS) & (core == 0))
    def _():
        load_own(o_hbm).start()

    @pl.when((y < SLABS) & (core == 1))
    def _():
        load_own(v_hbm).start()

    barrier = pltpu.get_barrier_semaphore()

    def greet_col(d, _):
        pl.semaphore_signal(barrier, inc=1, device_id={"col": (col + d) % NTILE}, device_id_type=MESH)
        return 0

    def greet_y(d, _):
        pl.semaphore_signal(barrier, inc=1, device_id={"ri": (y + d) % NY}, device_id_type=MESH)
        return 0

    lax.fori_loop(1, NTILE, greet_col, 0)
    lax.fori_loop(1, NY, greet_y, 0)
    pl.semaphore_signal(barrier, inc=1, device_id={"row": other}, device_id_type=MESH)

    loads[0].wait()
    loads[1].wait()
    place = lax.broadcasted_iota(jnp.int32, (8, NORB), 1)
    tile, pos = place // BS, place % BS
    live = jnp.zeros((8, NORB), jnp.int32)
    weight = jnp.zeros((8, NORB), jnp.int32)
    for t in range(NTILE):
        here = (tile == t) & (pos < fill_ref[t])
        live = jnp.where(here, 1, live)
        weight = jnp.where(here, mask_ref[col, t], weight)
    live_cols = live.astype(jnp.float32)[:1]
    live_rows = lax.broadcasted_iota(jnp.int32, (BS, 1), 0) < fill_ref[col]
    screen = (weight.astype(jnp.float32)[:1] * live_rows.astype(jnp.float32)).astype(jnp.bfloat16)

    def out_tile(i):
        turn, odd = i // 2, i % 2
        return (z + turn + odd) % 3 + 3 * ((half + 1 + odd) % 2)

    def in_tile(i):
        turn, odd = i % 3, i // 3
        return (z + 5 - turn + odd) % 3 + 3 * ((half + odd) % 2)

    def pack(i):
        at = out_tile(i)
        c_out[at] = c_in[:, at] * screen[None]

    def z_copy(to, at):
        rows = pl.ds(x * GROUP + at * BS, BS)
        return pltpu.make_async_remote_copy(
            src_ref=own, dst_ref=full.at[core, y, rows],
            send_sem=z_send.at[to], recv_sem=z_recv.at[at],
            device_id={"col": x * NZ + to}, device_id_type=MESH,
        )

    def own_z():
        return pltpu.make_async_copy(own, full.at[core, y, pl.ds(col * BS, BS)], load_sem.at[0])

    def y_copy(to, at):
        rows = pl.ds(x * GROUP, GROUP)
        return pltpu.make_async_remote_copy(
            src_ref=full.at[core, at, rows], dst_ref=full.at[core, at, rows],
            send_sem=y_send.at[to], recv_sem=y_recv.at[at],
            device_id={"ri": to}, device_id_type=MESH,
        )

    def x_copy(to, at, slab, mark=None):
        rows = pl.ds(at * GROUP, GROUP)
        return pltpu.make_async_remote_copy(
            src_ref=full.at[core, slab, rows], dst_ref=full.at[core, slab, rows],
            send_sem=x_send.at[to if mark is None else mark, slab], recv_sem=x_recv.at[at, slab],
            device_id={"col": to * NZ + z}, device_id_type=MESH,
        )

    def k_copy(part, at, slab):
        rows = pl.ds(part * GROUP, GROUP)
        return pltpu.make_async_remote_copy(
            src_ref=full.at[at, slab, rows], dst_ref=full.at[at, slab, rows],
            send_sem=k_send.at[part, slab], recv_sem=k_recv.at[part, slab],
            device_id={"row": other}, device_id_type=MESH,
        )

    def slab_at(turn):
        odd = turn % 2
        return (y + odd * (turn + 1) // 2 + (1 - odd) * (NY - turn // 2)) % NY

    def c_copy(to_x, to_z, at_x, at_z):
        return pltpu.make_async_remote_copy(
            src_ref=c_out.at[to_z, to_x], dst_ref=c_got.at[at_z, at_x],
            send_sem=send_sem.at[to_z, to_x], recv_sem=recv_sem.at[at_z, at_x],
            device_id={"col": to_x * NZ + to_z}, device_id_type=MESH,
        )

    def send_tile(i):
        to_z = out_tile(i)

        def send(d, _):
            to_x = (x + d) % NX

            @pl.when((d > 0) | (to_z != z))
            def _():
                c_copy(to_x, to_z, x, z).start()

            return 0

        lax.fori_loop(0, NX, send, 0)

    loads[2].wait()
    lax.fori_loop(0, NZ, lambda i, _: (pack(i), 0)[1], 0)
    pl.semaphore_wait(barrier, NTILE + NY - 1)

    @pl.when(y < SLABS)
    def _():
        def send(d, _):
            z_copy((z + d) % NZ, z).start()
            return 0

        load_own(o_hbm).wait()
        own_z().start()
        lax.fori_loop(1, NZ, send, 0)

    lax.fori_loop(0, NZ - 1, lambda i, _: (send_tile(jnp.where(i < LATE, i, NZ - 1)), 0)[1], 0)
    keep = pltpu.make_async_copy(c_out.at[z, x], c_got.at[z, x], load_sem.at[1])
    keep.start()

    @pl.when(y < SLABS)
    def _():
        def take(d, _):
            z_copy(z, (z + d) % NZ).wait_recv()
            return 0

        def send(d, _):
            y_copy((y + d) % NY, y).start()
            return 0

        own_z().wait()
        lax.fori_loop(1, NZ, take, 0)
        lax.fori_loop(1, NY, send, 0)

    def spread(turn, _):
        slab = slab_at(turn)

        @pl.when(slab < SLABS)
        def _():
            @pl.when(turn > 0)
            def _():
                y_copy(y, slab).wait_recv()

            x_copy((x + 1) % NX, x, slab).start()
            x_copy((x + 3) % NX, x, slab).start()
            k_copy(x, core, slab).start()

        return 0

    lax.fori_loop(0, NY, spread, 0)
    send_tile(LATE)

    def share(turn, _):
        slab = slab_at(turn)

        @pl.when(slab < SLABS)
        def _():
            even = slab % 2 == 0
            for part, beyond, forward in (
                ((x + 3) % NX, (x + 1) % NX, even),
                ((x + 1) % NX, (x + 3) % NX, jnp.logical_not(even)),
            ):
                x_copy(x, part, slab).wait_recv()

                @pl.when(forward)
                def _():
                    x_copy(beyond, part, slab, (x + 2) % NX).start()

                k_copy(part, core, slab).start()

        return 0

    def share_far(turn, _):
        slab = slab_at(turn)

        @pl.when(slab < SLABS)
        def _():
            part = (x + 2) % NX
            x_copy(x, part, slab).wait_recv()
            k_copy(part, core, slab).start()

        return 0

    lax.fori_loop(0, NY, share, 0)
    lax.fori_loop(0, NY, share_far, 0)

    def take_k(which):
        def take(i, _):
            k_copy(i // SLABS, which, i % SLABS).wait_recv()
            return 0

        lax.fori_loop(0, NX * SLABS, take, 0)

    @pl.when(core == 1)
    def _():
        take_k(0)

    occ = jnp.concatenate([full[0, slab] for slab in range(SLABS)], axis=1)
    keep.wait()

    def half_transform(i, _):
        at_z = in_tile(i)

        def take(d, _):
            at_x = (x + d) % NX

            @pl.when((d > 0) | (at_z != z))
            def _():
                c_copy(x, z, at_x, at_z).wait_recv()

            return 0

        lax.fori_loop(0, NX, take, 0)
        got = c_got[at_z].reshape(PART, NORB)
        done = jnp.dot(got, occ, preferred_element_type=jnp.float32).astype(jnp.bfloat16)
        for k in range(NX):
            half_done[pl.ds(k * GROUP + at_z * BS, BS), :] = done[k * BS:(k + 1) * BS]
        return 0

    lax.fori_loop(0, NZ, half_transform, 0)

    @pl.when(core == 0)
    def _():
        take_k(1)

    def store(k):
        rows = pl.ds(k * GROUP, GROUP)
        return pltpu.make_async_copy(done.at[rows], out_hbm.at[rows], load_sem.at[k])

    for k in range(NORB // GROUP):
        rows = pl.ds(k * GROUP, GROUP)
        virt = jnp.concatenate([full[1, slab, rows] for slab in range(SLABS)], axis=1)
        product = jnp.dot(virt, half_done[...], preferred_element_type=jnp.float32) * live_cols
        for t in range(NZ):
            at = lax.broadcasted_iota(jnp.int32, (BS, NORB), 0)
            kept = jnp.where(at < fill_ref[k * NZ + t], product[t * BS:(t + 1) * BS], 0.0)
            done[pl.ds(k * GROUP + t * BS, BS), :] = kept.astype(jnp.bfloat16)
        store(k).start()

    @pl.when(y < SLABS)
    def _():
        def left_z(d, _):
            z_copy((z + d) % NZ, z).wait_send()
            return 0

        def left_y(d, _):
            y_copy((y + d) % NY, y).wait_send()
            return 0

        lax.fori_loop(1, NZ, left_z, 0)
        lax.fori_loop(1, NY, left_y, 0)

    def left_slab(slab, _):
        def left_x(d, _):
            x_copy((x + d) % NX, x, slab).wait_send()
            return 0

        def left_k(part, _):
            k_copy(part, core, slab).wait_send()
            return 0

        lax.fori_loop(1, NX, left_x, 0)
        lax.fori_loop(0, NX, left_k, 0)
        return 0

    def left_c(i, _):
        to_z, to_x = i // NX, i % NX

        @pl.when((to_z != z) | (to_x != x))
        def _():
            c_copy(to_x, to_z, x, z).wait_send()

        return 0

    lax.fori_loop(0, SLABS, left_slab, 0)
    lax.fori_loop(0, NTILE, left_c, 0)
    for k in range(NORB // GROUP):
        store(k).wait()


def exchange(coulomb3, tile_mask, tile_fill, occ_density, virt_density):
    dma = pltpu.SemaphoreType.DMA
    bf16 = jnp.bfloat16
    return pl.pallas_call(
        exchange_kernel,
        out_shape=jax.ShapeDtypeStruct((NORB, NORB), bf16),
        in_specs=[pl.BlockSpec(memory_space=pltpu.HBM)] * 5,
        out_specs=pl.BlockSpec(memory_space=pltpu.HBM),
        scratch_shapes=[
            pltpu.SMEM((NTILE,), jnp.int32),
            pltpu.SMEM((NTILE, NTILE), jnp.int32),
            pltpu.VMEM((NX, NZ, BS, NORB), bf16),
            pltpu.VMEM((NZ, NX, BS, NORB), bf16),
            pltpu.VMEM((NZ, NX, BS, NORB), bf16),
            pltpu.VMEM((BS, 128), bf16),
            pltpu.VMEM((2, SLABS, NORB, 128), bf16),
            pltpu.VMEM((NORB, NORB), bf16),
            pltpu.VMEM((NORB, NORB), bf16),
            dma((5,)), dma((NZ, NX)), dma((NZ, NX)), dma((NZ,)), dma((NZ,)),
            dma((NY,)), dma((NY,)),
            dma((NX, SLABS)), dma((NX, SLABS)), dma((NX, SLABS)), dma((NX, SLABS)),
        ],
        compiler_params=pltpu.CompilerParams(
            collective_id=0, has_side_effects=True, vmem_limit_bytes=60 * 1024 * 1024
        ),
        name="exchange",
    )(tile_fill, tile_mask, coulomb3.reshape(NX, NZ, BS, NORB), occ_density, virt_density)


def on_device(coulomb3, tile_mask, tile_fill, occ_density, virt_density):
    return exchange(coulomb3, tile_mask, tile_fill, occ_density, virt_density)[None, None]


def solution(mesh):
    placed = (P(("row", "ri"), "col", None), P(), P(), P("col", None), P("col", None))
    return jax.shard_map(
        on_device,
        mesh=mesh,
        in_specs=placed,
        out_specs=P(("row", "ri"), "col", None, None),
        check_vma=False,
    )
```

```python
import jax
import jax.numpy as jnp
from jax import lax
from jax.experimental import pallas as pl
from jax.experimental.pallas import tpu as pltpu
from jax.sharding import PartitionSpec as P

MESH = pl.DeviceIdType.MESH
NX, NZ, NY = 4, 6, 8
BS, NTILE, NORB = 32, 24, 768
SLABS = NORB // 128
LATE = 4
BLOCK = 384
GROUP = NZ * BS
PART = NX * BS


def exchange_kernel(
    fill_hbm, mask_hbm, c_hbm, o_hbm, v_hbm, out_hbm,
    fill_ref, mask_ref, c_in, c_out, c_got, own, full, half_done, done,
    load_sem, send_sem, recv_sem, z_send, z_recv, y_send, y_recv, x_send, x_recv, k_send, k_recv,
):
    row, col, y = lax.axis_index("row"), lax.axis_index("col"), lax.axis_index("ri")
    x, z = col // NZ, col % NZ
    core = row % 2
    other = row + 1 - 2 * core
    half = z // 3

    loads = [
        pltpu.make_async_copy(fill_hbm, fill_ref, load_sem.at[0]),
        pltpu.make_async_copy(mask_hbm, mask_ref, load_sem.at[1]),
        pltpu.make_async_copy(c_hbm, c_in, load_sem.at[2]),
    ]
    for load in loads:
        load.start()

    def load_own(source):
        cols = pl.ds(pl.multiple_of(y * 128, 128), 128)
        return pltpu.make_async_copy(source.at[:, cols], own, load_sem.at[3])

    @pl.when((y < SLABS) & (core == 0))
    def _():
        load_own(o_hbm).start()

    @pl.when((y < SLABS) & (core == 1))
    def _():
        load_own(v_hbm).start()

    barrier = pltpu.get_barrier_semaphore()

    def greet_col(d, _):
        pl.semaphore_signal(barrier, inc=1, device_id={"col": (col + d) % NTILE}, device_id_type=MESH)
        return 0

    def greet_y(d, _):
        pl.semaphore_signal(barrier, inc=1, device_id={"ri": (y + d) % NY}, device_id_type=MESH)
        return 0

    lax.fori_loop(1, NTILE, greet_col, 0)
    lax.fori_loop(1, NY, greet_y, 0)
    pl.semaphore_signal(barrier, inc=1, device_id={"row": other}, device_id_type=MESH)

    loads[0].wait()
    loads[1].wait()
    place = lax.broadcasted_iota(jnp.int32, (8, NORB), 1)
    tile, pos = place // BS, place % BS
    live = jnp.zeros((8, NORB), jnp.int32)
    weight = jnp.zeros((8, NORB), jnp.int32)
    for t in range(NTILE):
        here = (tile == t) & (pos < fill_ref[t])
        live = jnp.where(here, 1, live)
        weight = jnp.where(here, mask_ref[col, t], weight)
    live_cols = live.astype(jnp.float32)[:1]
    live_rows = lax.broadcasted_iota(jnp.int32, (BS, 1), 0) < fill_ref[col]
    screen = (weight.astype(jnp.float32)[:1] * live_rows.astype(jnp.float32)).astype(jnp.bfloat16)

    def out_tile(i):
        turn, odd = i // 2, i % 2
        return (z + turn + odd) % 3 + 3 * ((half + 1 + odd) % 2)

    def in_tile(i):
        turn, odd = i % 3, i // 3
        return (z + 5 - turn + odd) % 3 + 3 * ((half + odd) % 2)

    def pack(i):
        at = out_tile(i)
        c_out[at] = c_in[:, at] * screen[None]

    def z_copy(to, at):
        rows = pl.ds(x * GROUP + at * BS, BS)
        return pltpu.make_async_remote_copy(
            src_ref=own, dst_ref=full.at[core, y, rows],
            send_sem=z_send.at[to], recv_sem=z_recv.at[at],
            device_id={"col": x * NZ + to}, device_id_type=MESH,
        )

    def own_z():
        return pltpu.make_async_copy(own, full.at[core, y, pl.ds(col * BS, BS)], load_sem.at[0])

    def y_copy(to, at):
        rows = pl.ds(x * GROUP, GROUP)
        return pltpu.make_async_remote_copy(
            src_ref=full.at[core, at, rows], dst_ref=full.at[core, at, rows],
            send_sem=y_send.at[to], recv_sem=y_recv.at[at],
            device_id={"ri": to}, device_id_type=MESH,
        )

    def x_copy(to, at, slab, mark=None):
        rows = pl.ds(at * GROUP, GROUP)
        return pltpu.make_async_remote_copy(
            src_ref=full.at[core, slab, rows], dst_ref=full.at[core, slab, rows],
            send_sem=x_send.at[to if mark is None else mark, slab], recv_sem=x_recv.at[at, slab],
            device_id={"col": to * NZ + z}, device_id_type=MESH,
        )

    def k_copy(part, at, slab):
        rows = pl.ds(part * GROUP, GROUP)
        return pltpu.make_async_remote_copy(
            src_ref=full.at[at, slab, rows], dst_ref=full.at[at, slab, rows],
            send_sem=k_send.at[part, slab], recv_sem=k_recv.at[part, slab],
            device_id={"row": other}, device_id_type=MESH,
        )

    def slab_at(turn):
        odd = turn % 2
        return (y + odd * (turn + 1) // 2 + (1 - odd) * (NY - turn // 2)) % NY

    def c_copy(to_x, to_z, at_x, at_z):
        return pltpu.make_async_remote_copy(
            src_ref=c_out.at[to_z, to_x], dst_ref=c_got.at[at_z, at_x],
            send_sem=send_sem.at[to_z, to_x], recv_sem=recv_sem.at[at_z, at_x],
            device_id={"col": to_x * NZ + to_z}, device_id_type=MESH,
        )

    def send_tile(i):
        to_z = out_tile(i)

        def send(d, _):
            to_x = (x + d) % NX

            @pl.when((d > 0) | (to_z != z))
            def _():
                c_copy(to_x, to_z, x, z).start()

            return 0

        lax.fori_loop(0, NX, send, 0)

    loads[2].wait()
    lax.fori_loop(0, NZ, lambda i, _: (pack(i), 0)[1], 0)
    pl.semaphore_wait(barrier, NTILE + NY - 1)

    @pl.when(y < SLABS)
    def _():
        def send(d, _):
            z_copy((z + d) % NZ, z).start()
            return 0

        load_own(o_hbm).wait()
        own_z().start()
        lax.fori_loop(1, NZ, send, 0)

    lax.fori_loop(0, NZ - 1, lambda i, _: (send_tile(jnp.where(i < LATE, i, NZ - 1)), 0)[1], 0)
    keep = pltpu.make_async_copy(c_out.at[z, x], c_got.at[z, x], load_sem.at[1])
    keep.start()

    @pl.when(y < SLABS)
    def _():
        def take(d, _):
            z_copy(z, (z + d) % NZ).wait_recv()
            return 0

        def send(d, _):
            y_copy((y + d) % NY, y).start()
            return 0

        own_z().wait()
        lax.fori_loop(1, NZ, take, 0)
        lax.fori_loop(1, NY, send, 0)

    def spread(turn, _):
        slab = slab_at(turn)

        @pl.when(slab < SLABS)
        def _():
            @pl.when(turn > 0)
            def _():
                y_copy(y, slab).wait_recv()

            x_copy((x + 1) % NX, x, slab).start()
            x_copy((x + 3) % NX, x, slab).start()
            k_copy(x, core, slab).start()

        return 0

    lax.fori_loop(0, NY, spread, 0)
    send_tile(LATE)

    def share(turn, _):
        slab = slab_at(turn)

        @pl.when(slab < SLABS)
        def _():
            even = slab % 2 == 0
            for part, beyond, forward in (
                ((x + 3) % NX, (x + 1) % NX, even),
                ((x + 1) % NX, (x + 3) % NX, jnp.logical_not(even)),
            ):
                x_copy(x, part, slab).wait_recv()

                @pl.when(forward)
                def _():
                    x_copy(beyond, part, slab, (x + 2) % NX).start()

                k_copy(part, core, slab).start()

        return 0

    def share_far(turn, _):
        slab = slab_at(turn)

        @pl.when(slab < SLABS)
        def _():
            part = (x + 2) % NX
            x_copy(x, part, slab).wait_recv()
            k_copy(part, core, slab).start()

        return 0

    lax.fori_loop(0, NY, share, 0)
    lax.fori_loop(0, NY, share_far, 0)

    def take_k(which):
        def take(i, _):
            k_copy(i // SLABS, which, i % SLABS).wait_recv()
            return 0

        lax.fori_loop(0, NX * SLABS, take, 0)

    @pl.when(core == 1)
    def _():
        take_k(0)

    occ = jnp.concatenate([full[0, slab] for slab in range(SLABS)], axis=1)
    keep.wait()

    def half_transform(i, _):
        at_z = in_tile(i)

        def take(d, _):
            at_x = (x + d) % NX

            @pl.when((d > 0) | (at_z != z))
            def _():
                c_copy(x, z, at_x, at_z).wait_recv()

            return 0

        lax.fori_loop(0, NX, take, 0)
        got = c_got[at_z].reshape(PART, NORB)
        done = jnp.dot(got, occ, preferred_element_type=jnp.float32).astype(jnp.bfloat16)
        for k in range(NX):
            half_done[pl.ds(k * GROUP + at_z * BS, BS), :] = done[k * BS:(k + 1) * BS]
        return 0

    lax.fori_loop(0, NZ, half_transform, 0)

    @pl.when(core == 0)
    def _():
        take_k(1)

    def store(k):
        rows = pl.ds(k * BLOCK, BLOCK)
        return pltpu.make_async_copy(done.at[rows], out_hbm.at[rows], load_sem.at[k])

    for k in range(NORB // BLOCK):
        rows = pl.ds(k * BLOCK, BLOCK)
        virt = jnp.concatenate([full[1, slab, rows] for slab in range(SLABS)], axis=1)
        product = jnp.dot(virt, half_done[...], preferred_element_type=jnp.float32) * live_cols
        for t in range(BLOCK // BS):
            at = lax.broadcasted_iota(jnp.int32, (BS, NORB), 0)
            kept = jnp.where(at < fill_ref[k * (BLOCK // BS) + t], product[t * BS:(t + 1) * BS], 0.0)
            done[pl.ds(k * BLOCK + t * BS, BS), :] = kept.astype(jnp.bfloat16)
        store(k).start()

    @pl.when(y < SLABS)
    def _():
        def left_z(d, _):
            z_copy((z + d) % NZ, z).wait_send()
            return 0

        def left_y(d, _):
            y_copy((y + d) % NY, y).wait_send()
            return 0

        lax.fori_loop(1, NZ, left_z, 0)
        lax.fori_loop(1, NY, left_y, 0)

    def left_slab(slab, _):
        def left_x(d, _):
            x_copy((x + d) % NX, x, slab).wait_send()
            return 0

        def left_k(part, _):
            k_copy(part, core, slab).wait_send()
            return 0

        lax.fori_loop(1, NX, left_x, 0)
        lax.fori_loop(0, NX, left_k, 0)
        return 0

    def left_c(i, _):
        to_z, to_x = i // NX, i % NX

        @pl.when((to_z != z) | (to_x != x))
        def _():
            c_copy(to_x, to_z, x, z).wait_send()

        return 0

    lax.fori_loop(0, SLABS, left_slab, 0)
    lax.fori_loop(0, NTILE, left_c, 0)
    for k in range(NORB // BLOCK):
        store(k).wait()


def exchange(coulomb3, tile_mask, tile_fill, occ_density, virt_density):
    dma = pltpu.SemaphoreType.DMA
    bf16 = jnp.bfloat16
    return pl.pallas_call(
        exchange_kernel,
        out_shape=jax.ShapeDtypeStruct((NORB, NORB), bf16),
        in_specs=[pl.BlockSpec(memory_space=pltpu.HBM)] * 5,
        out_specs=pl.BlockSpec(memory_space=pltpu.HBM),
        scratch_shapes=[
            pltpu.SMEM((NTILE,), jnp.int32),
            pltpu.SMEM((NTILE, NTILE), jnp.int32),
            pltpu.VMEM((NX, NZ, BS, NORB), bf16),
            pltpu.VMEM((NZ, NX, BS, NORB), bf16),
            pltpu.VMEM((NZ, NX, BS, NORB), bf16),
            pltpu.VMEM((BS, 128), bf16),
            pltpu.VMEM((2, SLABS, NORB, 128), bf16),
            pltpu.VMEM((NORB, NORB), bf16),
            pltpu.VMEM((NORB, NORB), bf16),
            dma((5,)), dma((NZ, NX)), dma((NZ, NX)), dma((NZ,)), dma((NZ,)),
            dma((NY,)), dma((NY,)),
            dma((NX, SLABS)), dma((NX, SLABS)), dma((NX, SLABS)), dma((NX, SLABS)),
        ],
        compiler_params=pltpu.CompilerParams(
            collective_id=0, has_side_effects=True, vmem_limit_bytes=60 * 1024 * 1024
        ),
        name="exchange",
    )(tile_fill, tile_mask, coulomb3.reshape(NX, NZ, BS, NORB), occ_density, virt_density)


def on_device(coulomb3, tile_mask, tile_fill, occ_density, virt_density):
    return exchange(coulomb3, tile_mask, tile_fill, occ_density, virt_density)[None, None]


def solution(mesh):
    placed = (P(("row", "ri"), "col", None), P(), P(), P("col", None), P("col", None))
    return jax.shard_map(
        on_device,
        mesh=mesh,
        in_specs=placed,
        out_specs=P(("row", "ri"), "col", None, None),
        check_vma=False,
    )
```
